128 devices in a mesh: dp: 128 (over x, z, y, core).
Axes of the slice: x: 4, y: 4, z: 4, core: 2. Of those that a mesh axis runs over, the one named last changes fastest.
Arguments:
- kv_pool: bfloat16 [16384, 64, 576], P('dp'), as said below
- queries: bfloat16 [3, 2048, 128, 576], P(None, 'dp'), as said below
- new_kv: bfloat16 [3, 2048, 576], P(None, 'dp'), as said below
- lengths: int32 [2048], replicated, may hold values from 1 to 512, as said below
- page_table: int32 [2048, 8], P('dp'), may hold values from 0 to 127, as said below
- mover_index: int32 [256], replicated, may hold values from 0 to 15, as said below
- mover_shift: int32 [2], replicated, may hold values from 1 to 127, as said below
- mover_slots: int32 [256, 8], replicated, may hold values from 0 to 7, as said below
Outputs:
- attended: bfloat16 [3, 2048, 128, 512], P(None, 'dp')
- arrived: bfloat16 [2048, 64, 576], P('dp')
The draws below stay inside these ranges and needn't reach their ends.
Inputs may be any that keep to these rules, and one draw needn't show every extreme that they name: `kv_pool`: the floats of the cache and of new tokens are of order one. Absorbed queries; some may point strongly at keys of their request. `new_kv`: of order one. `lengths`: some request holds exactly 512 tokens. `page_table`: the rows of one device's 16 requests together name each of its 128 local pages exactly once. `mover_index`: distinct within a device. `mover_shift`: the same for every device. `mover_slots`: each row is a permutation of 0 .. 7.
All inputs are finite; a program needn't handle non-finite values.
Results may differ from the reference program's by a relative error of at most 0.0035.
Values may be sent and summed in bfloat16 or wider, within the bound.
No kernel may reach another device: no remote copies, remote signals or barrier semaphores. Data moves between devices by JAX's collectives and lax.ppermute only.
A program may use at most 128 MiB of HBM per device.

```python
import jax
import jax.numpy as jnp
from jax import lax

HEADS = 128
KV_RANK = 512
ROPE = 64
R = 16
HP = 8
PAGE = 64
STEPS = 3
MIG = 2
OWNERS = 128
REQS = 2048
POOL = 16384


def draw_lengths(key, part):
    key = jax.random.fold_in(key, 11)
    ceiling_random_key, spread_key = jax.random.split(key)
    capacity = HP * PAGE
    ceiling = jax.random.randint(ceiling_random_key, (OWNERS, 1), capacity // 2, capacity + 1)
    floor_len = jnp.maximum(ceiling // 4, 1)
    random_bits = jax.random.randint(spread_key, (OWNERS, R), 0, 1 << 20)
    drawn = floor_len + random_bits % (ceiling - floor_len + 1)
    return drawn.reshape(-1).at[0].set(capacity).astype(jnp.int32)


def draw_page_table(key, part):
    key = jax.random.fold_in(key, 12)
    device_keys = jax.random.split(key, OWNERS)
    orders = jax.vmap(lambda one_key: jax.random.permutation(one_key, R * HP))(device_keys)
    return orders.reshape(REQS, HP).astype(jnp.int32)


def draw_mover_index(key, part):
    key = jax.random.fold_in(key, 13)
    device_keys = jax.random.split(key, OWNERS)
    orders = jax.vmap(lambda one_key: jax.random.permutation(one_key, R)[:MIG])(device_keys)
    return orders.reshape(OWNERS * MIG).astype(jnp.int32)


def draw_mover_shift(key, part):
    key = jax.random.fold_in(key, 24)
    shift_key, where_key = jax.random.split(key)
    shifts = jax.random.randint(shift_key, (MIG,), 1, OWNERS)
    widest = jax.random.randint(where_key, (), 0, MIG)
    shifts = jnp.where(jnp.arange(MIG, dtype=jnp.int32) == widest, OWNERS - 1, shifts)
    return shifts.astype(jnp.int32)


def draw_mover_slots(key, part):
    key = jax.random.fold_in(key, 15)
    mover_keys = jax.random.split(key, OWNERS * MIG)
    orders = jax.vmap(lambda one_key: jax.random.permutation(one_key, HP))(mover_keys)
    return orders.astype(jnp.int32)


def draw_kv_pool(key, part):
    key = jax.random.fold_in(key, 16)
    value_key = jax.random.fold_in(key, 0)
    shape = (POOL, PAGE, KV_RANK + ROPE)
    values = jax.random.normal(value_key, shape, jnp.float32)
    return values.astype(jnp.bfloat16)


def draw_new_kv(key, part):
    key = jax.random.fold_in(key, 17)
    shape = (STEPS, REQS, KV_RANK + ROPE)
    values = jax.random.normal(key, shape, jnp.float32)
    return values.astype(jnp.bfloat16)


def draw_queries(key, part):
    query_key = jax.random.fold_in(key, 18)
    value_key = jax.random.fold_in(query_key, 0)
    shape = (STEPS, REQS, HEADS, KV_RANK + ROPE)
    values = jax.random.normal(value_key, shape, jnp.float32)
    return values.astype(jnp.bfloat16)


def setup_inputs(seed: int = 0) -> dict:
    keys = jax.random.split(jax.random.key(seed), 9)
    kv_pool = draw_kv_pool(jax.random.fold_in(keys[8], 71), 0)
    queries = draw_queries(jax.random.fold_in(keys[8], 71), 0)
    new_kv = draw_new_kv(jax.random.fold_in(keys[8], 71), 0)
    lengths = draw_lengths(jax.random.fold_in(keys[8], 71), 0)
    page_table = draw_page_table(jax.random.fold_in(keys[8], 71), 0)
    mover_index = draw_mover_index(jax.random.fold_in(keys[8], 71), 0)
    mover_shift = draw_mover_shift(jax.random.fold_in(keys[8], 71), 0)
    mover_slots = draw_mover_slots(jax.random.fold_in(keys[8], 71), 0)
    return dict(kv_pool=kv_pool, queries=queries, new_kv=new_kv, lengths=lengths, page_table=page_table, mover_index=mover_index, mover_shift=mover_shift, mover_slots=mover_slots)


score_scale = 192.0 ** -0.5


def attend(cache_keys, cache_lengths, step_queries, tail_keys):
    keys_wide = cache_keys.astype(jnp.float32)
    values_wide = keys_wide[:, :, :KV_RANK]
    positions = jnp.arange(cache_keys.shape[1], dtype=jnp.int32)
    visible = positions[None, None, :] < cache_lengths[:, None, None]
    results = []
    for decode_step in range(STEPS):
        query_wide = step_queries[decode_step].astype(jnp.float32)
        tail_wide = tail_keys[: decode_step + 1].astype(jnp.float32)
        cache_scores = jnp.einsum("rhc,rtc->rht", query_wide, keys_wide) * score_scale
        cache_scores = jnp.where(visible, cache_scores, -jnp.inf)
        tail_scores = jnp.einsum("rhc,jrc->rhj", query_wide, tail_wide) * score_scale
        largest = jnp.maximum(jnp.max(cache_scores, axis=-1), jnp.max(tail_scores, axis=-1))[..., None]
        cache_weights = jnp.exp(cache_scores - largest)
        tail_weights = jnp.exp(tail_scores - largest)
        weight_total = jnp.sum(cache_weights, axis=-1) + jnp.sum(tail_weights, axis=-1)
        cache_rounded = lax.optimization_barrier(cache_weights.astype(jnp.bfloat16)).astype(jnp.float32)
        tail_rounded = lax.optimization_barrier(tail_weights.astype(jnp.bfloat16)).astype(jnp.float32)
        summed = jnp.einsum("rht,rtc->rhc", cache_rounded, values_wide)
        summed = summed + jnp.einsum("rhj,jrc->rhc", tail_rounded, tail_wide[:, :, :KV_RANK])
        results.append((summed / weight_total[..., None]).astype(jnp.bfloat16))
    return jnp.stack(results)


def reference(kv_pool, queries, new_kv, lengths, page_table, mover_index, mover_shift, mover_slots):
    device_pool = kv_pool.reshape(OWNERS, R * HP, PAGE, KV_RANK + ROPE)
    device_table = page_table.reshape(OWNERS, R, HP)
    device_lengths = lengths.reshape(OWNERS, R)
    device_queries = queries.reshape(STEPS, OWNERS, R, HEADS, KV_RANK + ROPE)
    device_tails = new_kv.reshape(STEPS, OWNERS, R, KV_RANK + ROPE)

    def one_device(owner):
        cache_keys = device_pool[owner][device_table[owner].reshape(-1)].reshape(R, HP * PAGE, KV_RANK + ROPE)
        return attend(cache_keys, device_lengths[owner], device_queries[:, owner], device_tails[:, owner])

    per_device = lax.map(one_device, jnp.arange(OWNERS, dtype=jnp.int32))
    by_request = jnp.transpose(per_device, (1, 0, 2, 3, 4)).reshape(STEPS, REQS, HEADS, KV_RANK)

    owners_all = jnp.arange(OWNERS, dtype=jnp.int32)
    mover_rank = jnp.arange(MIG, dtype=jnp.int32)
    source_requests = (owners_all[:, None] * R + mover_index.reshape(OWNERS, MIG)).reshape(-1)
    target_owner = (owners_all[:, None] + mover_shift[None, :]) % OWNERS
    target_slots = (target_owner * R + mover_index[target_owner * MIG + mover_rank[None, :]]).reshape(-1)
    attended = by_request.at[:, target_slots].set(by_request[:, source_requests])

    page_ids = ((source_requests // R) * (R * HP))[:, None] + page_table[source_requests]
    moving = kv_pool[page_ids.reshape(-1)].reshape(OWNERS * MIG, HP, PAGE, KV_RANK + ROPE)
    live_pages = jnp.arange(HP, dtype=jnp.int32)[None, :] * PAGE < lengths[source_requests][:, None]
    moving = jnp.where(live_pages[:, :, None, None], moving, jnp.zeros((), moving.dtype))
    inverse = jnp.argsort(mover_slots, axis=1).astype(jnp.int32)
    placed = jnp.take_along_axis(moving, inverse[:, :, None, None], axis=1)
    placed = placed.reshape(OWNERS, MIG, HP, PAGE, KV_RANK + ROPE)
    anchor = (owners_all[:, None] - mover_shift[None, :]) % OWNERS
    arrived = placed[anchor, mover_rank[None, :]].reshape(OWNERS * MIG * HP, PAGE, KV_RANK + ROPE)
    return attended, arrived
```

```python
import functools

import jax
import jax.numpy as jnp
from jax import lax
from jax.experimental import pallas as pl
from jax.experimental.pallas import tpu as pltpu
from jax.sharding import PartitionSpec as P

KV_RANK = 512
ROPE = 64
WIDTH = KV_RANK + ROPE
HEADS = 128
STEPS = 3
REQUESTS = 16
PAGES = 8
TOKENS = 64
KEYS = PAGES * TOKENS
MOVERS = 2
LANES = 128
GROUP = 16
PAIR_ROWS = 2 * REQUESTS * PAGES
PAGE_ROWS = KEYS * WIDTH // LANES
ANSWER_ROWS = STEPS * HEADS * KV_RANK // LANES
PAYLOAD_ROWS = PAGE_ROWS + ANSWER_ROWS
VMEM_BYTES = 56 * 1024 * 1024

LOG2_E = 1.4426950408889634

score_scale = 192.0 ** (-0.5)


def near_mover(shift):
    ways = []
    for i in range(MOVERS):
        even = ((shift[i] + 1) >> 1) & 63
        ways.append(jnp.minimum(even, 64 - even))
    return jnp.where(ways[0] < ways[1], 0, 1)


def slot_mover(slot, shift):
    near = near_mover(shift)
    return near if slot == 1 else 1 - near


def slot_request(slot, me, index, shift):
    return index[me[0] * MOVERS + slot_mover(slot, shift)]


def score(keys, visible, tail, query):
    scores = jnp.dot(keys, query, preferred_element_type=jnp.float32)
    scores = jnp.where(jnp.concatenate([visible] * STEPS, axis=1), scores, -jnp.inf)
    tail_scores = jnp.dot(tail, query, preferred_element_type=jnp.float32)
    tail_row = lax.broadcasted_iota(jnp.int32, tail_scores.shape, 0)
    step = lax.broadcasted_iota(jnp.int32, tail_scores.shape, 1) >> 7
    tail_scores = jnp.where(tail_row <= step, tail_scores, -jnp.inf)
    return jnp.concatenate([scores, tail_scores], axis=0)


def answer_of(scores, values, tail_values):
    largest = jnp.max(scores, axis=0, keepdims=True)
    weights = jnp.exp2((scores - largest) * (score_scale * LOG2_E))
    share = 1.0 / jnp.sum(weights, axis=0, keepdims=True)
    rounded = weights.astype(jnp.bfloat16)
    contract = (((0,), (0,)), ((), ()))
    summed = lax.dot_general(
        rounded[:KEYS], values, contract, preferred_element_type=jnp.float32
    ) + lax.dot_general(rounded[KEYS:], tail_values, contract, preferred_element_type=jnp.float32)
    columns = [
        jnp.transpose(jnp.broadcast_to(share[:, s * HEADS : (s + 1) * HEADS], (HEADS, HEADS)))[:, :1]
        for s in range(STEPS)
    ]
    return (summed * jnp.concatenate(columns, axis=0)).astype(jnp.bfloat16)


def tail_rows(tails, request):
    row = lax.broadcasted_iota(jnp.int32, (16, STEPS * REQUESTS), 0)
    column = lax.broadcasted_iota(jnp.int32, (16, STEPS * REQUESTS), 1)
    pick = jnp.where(column == row * REQUESTS + request, 1.0, 0.0).astype(jnp.bfloat16)
    return jnp.dot(pick, tails, preferred_element_type=jnp.float32).astype(jnp.bfloat16)


def joined(query_ref):
    return jnp.concatenate([query_ref[s, 0] for s in range(STEPS)], axis=1)


def gathering_kernel(
    me,
    lengths,
    table,
    index,
    shift,
    slots,
    pool,
    table_block,
    query0,
    query1,
    tails,
    keys,
    out0,
    out1,
    far_even,
    near_low,
    near_high,
    far_odd,
    near_odd,
    select,
    leaving,
):
    group = pl.program_id(0)
    movers = [slot_mover(k, shift) for k in range(MOVERS)]
    requests = [index[me[0] * MOVERS + m] for m in movers]
    spans = [lengths[me[0] * REQUESTS + r] for r in requests]
    places = [[slots[j, me[0] * MOVERS + m] for j in range(PAGES)] for m in movers]

    @pl.when(group == 0)
    def _():
        far, near = shift[movers[0]], shift[movers[1]]
        even = (((near + 1) >> 1) & 63) + 4
        far_even[0] = far >> 1
        near_low[0] = even & 7
        near_high[0] = (even >> 3) & 7
        far_odd[0] = far & 1
        near_odd[0] = near & 1

        row = lax.broadcasted_iota(jnp.int32, (PAIR_ROWS, 1), 0) & ~PAGES
        owner = lax.broadcasted_iota(jnp.int32, (PAIR_ROWS, REQUESTS), 0) >> 4
        mine = owner == lax.broadcasted_iota(jnp.int32, (PAIR_ROWS, REQUESTS), 1)
        numbers = lax.dot_general(
            jnp.where(mine, 1.0, 0.0).astype(jnp.bfloat16),
            table_block[...].astype(jnp.float32).astype(jnp.bfloat16),
            (((1,), (1,)), ((), ())),
            preferred_element_type=jnp.float32,
        )
        place = lax.broadcasted_iota(jnp.int32, (PAIR_ROWS, PAGES), 0) & 7
        chosen = place == lax.broadcasted_iota(jnp.int32, (PAIR_ROWS, PAGES), 1)
        page = jnp.sum(jnp.where(chosen, numbers, 0.0), axis=1, keepdims=True).astype(jnp.int32)
        for k in range(MOVERS):
            for j in range(PAGES):
                number = jnp.where(j * TOKENS < spans[k], table[j, requests[k]], -1)
                here = row == requests[k] * (2 * PAGES) + places[k][j]
                page = jnp.where(here, number, page)
        column = lax.broadcasted_iota(jnp.int32, (PAIR_ROWS, 2 * LANES), 1)
        token = (lax.broadcasted_iota(jnp.int32, (PAIR_ROWS, 2 * LANES), 0) >> 3) & 1
        hit = ((column & 127) == page) & (token == column >> 7)
        select[...] = jnp.where(hit, 1.0, 0.0).astype(jnp.bfloat16)

    for u in range(GROUP // 2):
        got = lax.dot_general(
            select[...],
            jnp.concatenate([pool[2 * u], pool[2 * u + 1]], axis=1),
            (((1,), (1,)), ((), ())),
            preferred_element_type=jnp.float32,
        )
        keys[:, u * 16 : (u + 1) * 16, :] = got.reshape(REQUESTS, 16, WIDTH).astype(jnp.bfloat16)
    start = pl.multiple_of(group * (GROUP * PAGES), GROUP * PAGES)
    for k in range(MOVERS):
        leaving[k, pl.ds(start, GROUP * PAGES), :] = keys[requests[k]]

    @pl.when(group == TOKENS // GROUP - 1)
    def _():
        row = lax.broadcasted_iota(jnp.int32, (KEYS, LANES), 0)
        scores, extra = [], []
        for k, query in enumerate((query0, query1)):
            spare = spans[k] - (row >> 3)
            first = jnp.zeros((PAGES, LANES), jnp.int32)
            page_row = lax.broadcasted_iota(jnp.int32, (PAGES, LANES), 0)
            for j in range(PAGES):
                first = jnp.where(page_row == places[k][j], j * TOKENS, first)
            visible = (jnp.broadcast_to(first, (TOKENS, PAGES, LANES)).reshape(KEYS, LANES)) < spare
            extra.append(tail_rows(tails[...], requests[k]))
            scores.append(score(leaving[k], visible, extra[k], joined(query)))
        for k, out in enumerate((out0, out1)):
            for c in range(KV_RANK // LANES):
                out[c * KEYS : (c + 1) * KEYS] = leaving[k, :, c * LANES : (c + 1) * LANES]
            rope = leaving[k, :, KV_RANK:]
            out[4 * KEYS : PAGE_ROWS] = jnp.concatenate(
                [rope[: KEYS // 2], rope[KEYS // 2 :]], axis=1
            )
            answer = answer_of(scores[k], leaving[k, :, :KV_RANK], extra[k][:, :KV_RANK])
            for s in range(STEPS):
                for c in range(KV_RANK // LANES):
                    start = PAGE_ROWS + (s * 4 + c) * HEADS
                    out[start : start + HEADS] = answer[
                        s * HEADS : (s + 1) * HEADS, c * LANES : (c + 1) * LANES
                    ]


def gathering(scalars, pool, table, queries, tails):
    def query_spec(slot):
        return pl.BlockSpec(
            (STEPS, 1, WIDTH, HEADS),
            lambda i, me, lengths, table, index, shift, slots: (
                0,
                slot_request(slot, me, index, shift),
                0,
                0,
            ),
        )

    payload = jax.ShapeDtypeStruct((PAYLOAD_ROWS, LANES), jnp.bfloat16)
    number = jax.ShapeDtypeStruct((1,), jnp.int32)
    whole = pl.BlockSpec((PAYLOAD_ROWS, LANES), lambda i, *_: (0, 0))
    return pl.pallas_call(
        gathering_kernel,
        grid_spec=pltpu.PrefetchScalarGridSpec(
            num_scalar_prefetch=6,
            grid=(TOKENS // GROUP,),
            in_specs=[
                pl.BlockSpec((GROUP, WIDTH, LANES), lambda i, *_: (i, 0, 0)),
                pl.BlockSpec((PAGES, REQUESTS), lambda i, *_: (0, 0)),
                query_spec(0),
                query_spec(1),
                pl.BlockSpec((STEPS * REQUESTS, WIDTH), lambda i, *_: (0, 0)),
            ],
            out_specs=[
                pl.BlockSpec((REQUESTS, GROUP * PAGES, WIDTH), lambda i, *_: (0, i, 0)),
                whole,
                whole,
            ]
            + [pl.BlockSpec(memory_space=pltpu.SMEM)] * 5,
            scratch_shapes=[
                pltpu.VMEM((PAIR_ROWS, 2 * LANES), jnp.bfloat16),
                pltpu.VMEM((MOVERS, KEYS, WIDTH), jnp.bfloat16),
            ],
        ),
        out_shape=[
            jax.ShapeDtypeStruct((REQUESTS, KEYS, WIDTH), jnp.bfloat16),
            payload,
            payload,
        ]
        + [number] * 5,
        compiler_params=pltpu.CompilerParams(vmem_limit_bytes=VMEM_BYTES),
        cost_estimate=pl.CostEstimate(
            flops=4_000_000_000, bytes_accessed=24_000_000, transcendentals=400_000
        ),
        name="gathering",
    )(*scalars, pool, table, queries, queries, tails)


STAYING = REQUESTS - MOVERS


STAYING_STEPS = STAYING // 2


def staying_request(i, me, index):
    first, second = index[me[0] * MOVERS], index[me[0] * MOVERS + 1]
    low, high = jnp.minimum(first, second), jnp.maximum(first, second)
    request = i + jnp.where(i >= low, 1, 0)
    return request + jnp.where(request >= high, 1, 0)


def staying_kernel(
    me, lengths, index, keys0, keys1, query0, query1, tails, out, extras, answers, sent
):
    i = pl.program_id(0)
    slot = i % 2

    def leave(step, half):
        return pltpu.make_async_copy(
            answers.at[step % 2, half],
            out.at[:, staying_request(2 * step + half, me, index)],
            sent.at[step % 2, half],
        )

    @pl.when(i == 0)
    def _():
        row = lax.broadcasted_iota(jnp.int32, (16 * REQUESTS, STEPS * REQUESTS), 0)
        column = lax.broadcasted_iota(jnp.int32, (16 * REQUESTS, STEPS * REQUESTS), 1)
        hit = column == ((row & 15) << 4) + (row >> 4)
        pick = jnp.where(hit, 1.0, 0.0).astype(jnp.bfloat16)
        got = jnp.dot(pick, tails[...], preferred_element_type=jnp.float32)
        extras[...] = got.reshape(REQUESTS, 16, WIDTH).astype(jnp.bfloat16)

    @pl.when(i >= 2)
    def _():
        for half in range(2):
            leave(i - 2, half).wait()

    row = lax.broadcasted_iota(jnp.int32, (KEYS, LANES), 0)
    positions = ((row & 7) << 6) + (row >> 3)
    for half, (keys, query) in enumerate(((keys0, query0), (keys1, query1))):
        request = staying_request(2 * i + half, me, index)
        extra = extras[request]
        visible = positions < lengths[me[0] * REQUESTS + request]
        scores = score(keys[0], visible, extra, joined(query))
        answer = answer_of(scores, keys[0, :, :KV_RANK], extra[:, :KV_RANK])
        answers[slot, half] = answer.reshape(STEPS, HEADS, KV_RANK)
    for half in range(2):
        leave(i, half).start()

    @pl.when(i == STAYING_STEPS - 1)
    def _():
        for step in range(STAYING_STEPS - 2, STAYING_STEPS):
            for half in range(2):
                leave(step, half).wait()


def staying(scalars, keys, queries, tails):
    def key_spec(half):
        return pl.BlockSpec(
            (1, KEYS, WIDTH),
            lambda i, me, lengths, index: (staying_request(2 * i + half, me, index), 0, 0),
        )

    def query_spec(half):
        return pl.BlockSpec(
            (STEPS, 1, WIDTH, HEADS),
            lambda i, me, lengths, index: (0, staying_request(2 * i + half, me, index), 0, 0),
        )

    return pl.pallas_call(
        staying_kernel,
        grid_spec=pltpu.PrefetchScalarGridSpec(
            num_scalar_prefetch=3,
            grid=(STAYING_STEPS,),
            in_specs=[
                key_spec(0),
                key_spec(1),
                query_spec(0),
                query_spec(1),
                pl.BlockSpec((STEPS * REQUESTS, WIDTH), lambda i, *_: (0, 0)),
            ],
            out_specs=pl.BlockSpec(memory_space=pl.ANY),
            scratch_shapes=[
                pltpu.VMEM((REQUESTS, 16, WIDTH), jnp.bfloat16),
                pltpu.VMEM((2, 2, STEPS, HEADS, KV_RANK), jnp.bfloat16),
                pltpu.SemaphoreType.DMA((2, 2)),
            ],
        ),
        out_shape=jax.ShapeDtypeStruct((STEPS, REQUESTS, HEADS, KV_RANK), jnp.bfloat16),
        compiler_params=pltpu.CompilerParams(vmem_limit_bytes=VMEM_BYTES),
        cost_estimate=pl.CostEstimate(
            flops=7_000_000_000, bytes_accessed=21_000_000, transcendentals=3_000_000
        ),
        name="staying",
    )(*scalars, keys, keys, queries, queries, tails)


def landing_kernel(me, index, shift, far, near, old, arrived, attended):
    del me, index, shift, old
    for k, got in enumerate((far, near)):

        @pl.when(pl.program_id(0) == k)
        def _(got=got):
            row = lax.broadcasted_iota(jnp.int32, (KEYS, KEYS), 0)
            column = lax.broadcasted_iota(jnp.int32, (KEYS, KEYS), 1)
            hit = column == ((row & 63) << 3) + (row >> 6)
            by_page = jnp.where(hit, 1.0, 0.0).astype(jnp.bfloat16)

            def turned(rows):
                block = jnp.dot(by_page, rows, preferred_element_type=jnp.float32)
                return block.astype(jnp.bfloat16).reshape(PAGES, TOKENS, rows.shape[1])

            arrived[:, :, :KV_RANK] = turned(
                jnp.concatenate(
                    [got[c * KEYS : (c + 1) * KEYS] for c in range(KV_RANK // LANES)], axis=1
                )
            )
            rope = got[4 * KEYS : PAGE_ROWS]
            arrived[:, :, KV_RANK:] = turned(
                jnp.concatenate([rope[:, :ROPE], rope[:, ROPE:]], axis=0)
            )
            for s in range(STEPS):
                for c in range(KV_RANK // LANES):
                    start = PAGE_ROWS + (s * 4 + c) * HEADS
                    attended[s, 0, :, c * LANES : (c + 1) * LANES] = got[start : start + HEADS]


def landing(scalars, far, near, attended):
    whole = pl.BlockSpec((PAYLOAD_ROWS, LANES), lambda i, *_: (0, 0))

    def mover(i, shift):
        last = near_mover(shift)
        return jnp.where(i == 1, last, 1 - last)

    return pl.pallas_call(
        landing_kernel,
        grid_spec=pltpu.PrefetchScalarGridSpec(
            num_scalar_prefetch=3,
            grid=(MOVERS,),
            in_specs=[whole] * 2 + [pl.BlockSpec(memory_space=pl.ANY)],
            out_specs=[
                pl.BlockSpec(
                    (PAGES, TOKENS, WIDTH), lambda i, me, index, shift: (mover(i, shift), 0, 0)
                ),
                pl.BlockSpec(
                    (STEPS, 1, HEADS, KV_RANK),
                    lambda i, me, index, shift: (
                        0,
                        index[me[0] * MOVERS + mover(i, shift)],
                        0,
                        0,
                    ),
                ),
            ],
        ),
        out_shape=[
            jax.ShapeDtypeStruct((MOVERS * PAGES, TOKENS, WIDTH), jnp.bfloat16),
            jax.ShapeDtypeStruct(attended.shape, attended.dtype),
        ],
        input_output_aliases={5: 1},
        compiler_params=pltpu.CompilerParams(vmem_limit_bytes=VMEM_BYTES),
        cost_estimate=pl.CostEstimate(flops=0, bytes_accessed=6_000_000, transcendentals=0),
        name="landing",
    )(*scalars, far, near, attended)


def moved(block, distance):
    count = lax.axis_size("dp")
    if distance % count == 0:
        return block
    return lax.ppermute(block, "dp", [(i, (i + distance) % count) for i in range(count)])


def moved_by(block, choice, distances):
    branches = [functools.partial(moved, distance=d) for d in distances]
    return lax.switch(choice.reshape(()), branches, block)


def shards(kv_pool, queries, new_kv, lengths, page_table, mover_index, mover_shift, mover_slots):
    me = lax.axis_index("dp").reshape(1)
    pool = jnp.transpose(kv_pool, (1, 2, 0))
    turned = jnp.transpose(queries, (0, 1, 3, 2))
    tails = new_kv.reshape(STEPS * REQUESTS, WIDTH)
    keys, far, near, far_even, near_low, near_high, far_odd, near_odd = gathering(
        (me, lengths, page_table.T, mover_index, mover_shift, mover_slots.T),
        pool,
        page_table.T,
        turned,
        tails,
    )
    far_next = moved(far, 1)
    near_next = moved(near, -1)
    attended = staying((me, lengths, mover_index), keys, turned, tails)
    far_next, near_next, attended = lax.optimization_barrier((far_next, near_next, attended))
    far = jnp.where(far_odd == 1, far_next, far)
    near = jnp.where(near_odd == 1, near_next, near)
    near = moved_by(near, near_low, [2 * (k - 4) for k in range(8)])
    near = moved_by(near, near_high, [16 * k for k in range(8)])
    far_even = far_even.reshape(())
    far = moved_by(far, jnp.maximum(far_even - 31, 0), [0] + [2 * k for k in range(32, 64)])
    far = moved_by(far, jnp.where(far_even < 32, far_even, 0), [2 * k for k in range(32)])
    arrived, attended = landing((me, mover_index, mover_shift), far, near, attended)
    return attended, arrived


def solution(mesh):
    in_specs = (
        P("dp", None, None),
        P(None, "dp", None, None),
        P(None, "dp", None),
        P(),
        P("dp", None),
        P(),
        P(),
        P(),
    )
    out_specs = (P(None, "dp", None, None), P("dp", None, None))
    return jax.shard_map(shards, mesh=mesh, in_specs=in_specs, out_specs=out_specs, check_vma=False)
```

```python
import functools

import jax
import jax.numpy as jnp
from jax import lax
from jax.experimental import pallas as pl
from jax.experimental.pallas import tpu as pltpu
from jax.sharding import PartitionSpec as P

KV_RANK = 512
ROPE = 64
WIDTH = KV_RANK + ROPE
HEADS = 128
STEPS = 3
REQUESTS = 16
PAGES = 8
TOKENS = 64
KEYS = PAGES * TOKENS
MOVERS = 2
LANES = 128
GROUP = 16
PAIR_ROWS = 2 * REQUESTS * PAGES
FAR_THIRDS = 21
PAGE_ROWS = KEYS * WIDTH // LANES
ANSWER_ROWS = STEPS * HEADS * KV_RANK // LANES
PAYLOAD_ROWS = PAGE_ROWS + ANSWER_ROWS
VMEM_BYTES = 56 * 1024 * 1024

LOG2_E = 1.4426950408889634

score_scale = 192.0 ** (-0.5)


def thirds(shift):
    back = jnp.where(shift > 64, 1, 0)
    third = lax.div(shift + 1 + back, 3) - 43 * back
    return third, shift - 128 * back - 3 * third


def near_mover(shift):
    ways = [jnp.abs(thirds(shift[i])[0]) for i in range(MOVERS)]
    return jnp.where(ways[0] < ways[1], 0, 1)


def slot_mover(slot, shift):
    near = near_mover(shift)
    return near if slot == 1 else 1 - near


def slot_request(slot, me, index, shift):
    return index[me[0] * MOVERS + slot_mover(slot, shift)]


def score(keys, visible, tail, query):
    scores = jnp.dot(keys, query, preferred_element_type=jnp.float32)
    scores = jnp.where(jnp.concatenate([visible] * STEPS, axis=1), scores, -jnp.inf)
    tail_scores = jnp.dot(tail, query, preferred_element_type=jnp.float32)
    tail_row = lax.broadcasted_iota(jnp.int32, tail_scores.shape, 0)
    step = lax.broadcasted_iota(jnp.int32, tail_scores.shape, 1) >> 7
    tail_scores = jnp.where(tail_row <= step, tail_scores, -jnp.inf)
    return jnp.concatenate([scores, tail_scores], axis=0)


def answer_of(scores, values, tail_values):
    largest = jnp.max(scores, axis=0, keepdims=True)
    weights = jnp.exp2((scores - largest) * (score_scale * LOG2_E))
    share = 1.0 / jnp.sum(weights, axis=0, keepdims=True)
    rounded = weights.astype(jnp.bfloat16)
    contract = (((0,), (0,)), ((), ()))
    summed = lax.dot_general(
        rounded[:KEYS], values, contract, preferred_element_type=jnp.float32
    ) + lax.dot_general(rounded[KEYS:], tail_values, contract, preferred_element_type=jnp.float32)
    columns = [
        jnp.transpose(jnp.broadcast_to(share[:, s * HEADS : (s + 1) * HEADS], (HEADS, HEADS)))[:, :1]
        for s in range(STEPS)
    ]
    return (summed * jnp.concatenate(columns, axis=0)).astype(jnp.bfloat16)


def tail_rows(tails, request):
    row = lax.broadcasted_iota(jnp.int32, (16, STEPS * REQUESTS), 0)
    column = lax.broadcasted_iota(jnp.int32, (16, STEPS * REQUESTS), 1)
    pick = jnp.where(column == row * REQUESTS + request, 1.0, 0.0).astype(jnp.bfloat16)
    return jnp.dot(pick, tails, preferred_element_type=jnp.float32).astype(jnp.bfloat16)


def joined(query_ref):
    return jnp.concatenate([query_ref[s, 0] for s in range(STEPS)], axis=1)


def gathering_kernel(
    me,
    lengths,
    table,
    index,
    shift,
    slots,
    pool,
    table_block,
    query0,
    query1,
    tails,
    keys,
    out,
    far_third,
    near_third,
    select,
    leaving,
):
    group = pl.program_id(0)
    movers = [slot_mover(k, shift) for k in range(MOVERS)]
    requests = [index[me[0] * MOVERS + m] for m in movers]
    spans = [lengths[me[0] * REQUESTS + r] for r in requests]
    places = [[slots[j, me[0] * MOVERS + m] for j in range(PAGES)] for m in movers]

    @pl.when(group == 0)
    def _():
        far_third[0] = thirds(shift[movers[0]])[0] + FAR_THIRDS
        near_third[0] = thirds(shift[movers[1]])[0] + FAR_THIRDS

        row = lax.broadcasted_iota(jnp.int32, (PAIR_ROWS, 1), 0) & ~PAGES
        owner = lax.broadcasted_iota(jnp.int32, (PAIR_ROWS, REQUESTS), 0) >> 4
        mine = owner == lax.broadcasted_iota(jnp.int32, (PAIR_ROWS, REQUESTS), 1)
        numbers = lax.dot_general(
            jnp.where(mine, 1.0, 0.0).astype(jnp.bfloat16),
            table_block[...].astype(jnp.float32).astype(jnp.bfloat16),
            (((1,), (1,)), ((), ())),
            preferred_element_type=jnp.float32,
        )
        place = lax.broadcasted_iota(jnp.int32, (PAIR_ROWS, PAGES), 0) & 7
        chosen = place == lax.broadcasted_iota(jnp.int32, (PAIR_ROWS, PAGES), 1)
        page = jnp.sum(jnp.where(chosen, numbers, 0.0), axis=1, keepdims=True).astype(jnp.int32)
        for k in range(MOVERS):
            for j in range(PAGES):
                number = jnp.where(j * TOKENS < spans[k], table[j, requests[k]], -1)
                here = row == requests[k] * (2 * PAGES) + places[k][j]
                page = jnp.where(here, number, page)
        column = lax.broadcasted_iota(jnp.int32, (PAIR_ROWS, 2 * LANES), 1)
        token = (lax.broadcasted_iota(jnp.int32, (PAIR_ROWS, 2 * LANES), 0) >> 3) & 1
        hit = ((column & 127) == page) & (token == column >> 7)
        select[...] = jnp.where(hit, 1.0, 0.0).astype(jnp.bfloat16)

    for u in range(GROUP // 2):
        got = lax.dot_general(
            select[...],
            jnp.concatenate([pool[2 * u], pool[2 * u + 1]], axis=1),
            (((1,), (1,)), ((), ())),
            preferred_element_type=jnp.float32,
        )
        keys[:, u * 16 : (u + 1) * 16, :] = got.reshape(REQUESTS, 16, WIDTH).astype(jnp.bfloat16)
    start = pl.multiple_of(group * (GROUP * PAGES), GROUP * PAGES)
    for k in range(MOVERS):
        leaving[k, pl.ds(start, GROUP * PAGES), :] = keys[requests[k]]

    @pl.when(group == TOKENS // GROUP - 1)
    def _():
        row = lax.broadcasted_iota(jnp.int32, (KEYS, LANES), 0)
        scores, extra = [], []
        for k, query in enumerate((query0, query1)):
            spare = spans[k] - (row >> 3)
            first = jnp.zeros((PAGES, LANES), jnp.int32)
            page_row = lax.broadcasted_iota(jnp.int32, (PAGES, LANES), 0)
            for j in range(PAGES):
                first = jnp.where(page_row == places[k][j], j * TOKENS, first)
            visible = (jnp.broadcast_to(first, (TOKENS, PAGES, LANES)).reshape(KEYS, LANES)) < spare
            extra.append(tail_rows(tails[...], requests[k]))
            scores.append(score(leaving[k], visible, extra[k], joined(query)))
        for k in range(MOVERS):
            for c in range(KV_RANK // LANES):
                out[k, c * KEYS : (c + 1) * KEYS] = leaving[k, :, c * LANES : (c + 1) * LANES]
            rope = leaving[k, :, KV_RANK:]
            out[k, 4 * KEYS : PAGE_ROWS] = jnp.concatenate(
                [rope[: KEYS // 2], rope[KEYS // 2 :]], axis=1
            )
            answer = answer_of(scores[k], leaving[k, :, :KV_RANK], extra[k][:, :KV_RANK])
            for s in range(STEPS):
                for c in range(KV_RANK // LANES):
                    start = PAGE_ROWS + (s * 4 + c) * HEADS
                    out[k, start : start + HEADS] = answer[
                        s * HEADS : (s + 1) * HEADS, c * LANES : (c + 1) * LANES
                    ]


def gathering(scalars, pool, table, queries, tails):
    def query_spec(slot):
        return pl.BlockSpec(
            (STEPS, 1, WIDTH, HEADS),
            lambda i, me, lengths, table, index, shift, slots: (
                0,
                slot_request(slot, me, index, shift),
                0,
                0,
            ),
        )

    number = jax.ShapeDtypeStruct((1,), jnp.int32)
    return pl.pallas_call(
        gathering_kernel,
        grid_spec=pltpu.PrefetchScalarGridSpec(
            num_scalar_prefetch=6,
            grid=(TOKENS // GROUP,),
            in_specs=[
                pl.BlockSpec((GROUP, WIDTH, LANES), lambda i, *_: (i, 0, 0)),
                pl.BlockSpec((PAGES, REQUESTS), lambda i, *_: (0, 0)),
                query_spec(0),
                query_spec(1),
                pl.BlockSpec((STEPS * REQUESTS, WIDTH), lambda i, *_: (0, 0)),
            ],
            out_specs=[
                pl.BlockSpec((REQUESTS, GROUP * PAGES, WIDTH), lambda i, *_: (0, i, 0)),
                pl.BlockSpec((MOVERS, PAYLOAD_ROWS, LANES), lambda i, *_: (0, 0, 0)),
            ]
            + [pl.BlockSpec(memory_space=pltpu.SMEM)] * 2,
            scratch_shapes=[
                pltpu.VMEM((PAIR_ROWS, 2 * LANES), jnp.bfloat16),
                pltpu.VMEM((MOVERS, KEYS, WIDTH), jnp.bfloat16),
            ],
        ),
        out_shape=[
            jax.ShapeDtypeStruct((REQUESTS, KEYS, WIDTH), jnp.bfloat16),
            jax.ShapeDtypeStruct((MOVERS, PAYLOAD_ROWS, LANES), jnp.bfloat16),
        ]
        + [number] * 2,
        compiler_params=pltpu.CompilerParams(vmem_limit_bytes=VMEM_BYTES),
        cost_estimate=pl.CostEstimate(
            flops=4_000_000_000, bytes_accessed=24_000_000, transcendentals=400_000
        ),
        name="gathering",
    )(*scalars, pool, table, queries, queries, tails)


STAYING = REQUESTS - MOVERS


STAYING_STEPS = STAYING // 2


def staying_request(i, me, index):
    first, second = index[me[0] * MOVERS], index[me[0] * MOVERS + 1]
    low, high = jnp.minimum(first, second), jnp.maximum(first, second)
    request = i + jnp.where(i >= low, 1, 0)
    return request + jnp.where(request >= high, 1, 0)


def staying_kernel(
    me, lengths, index, keys0, keys1, query0, query1, tails, out, extras, answers, sent
):
    i = pl.program_id(0)
    slot = i % 2

    def leave(step, half):
        return pltpu.make_async_copy(
            answers.at[step % 2, half],
            out.at[:, staying_request(2 * step + half, me, index)],
            sent.at[step % 2, half],
        )

    @pl.when(i == 0)
    def _():
        row = lax.broadcasted_iota(jnp.int32, (16 * REQUESTS, STEPS * REQUESTS), 0)
        column = lax.broadcasted_iota(jnp.int32, (16 * REQUESTS, STEPS * REQUESTS), 1)
        hit = column == ((row & 15) << 4) + (row >> 4)
        pick = jnp.where(hit, 1.0, 0.0).astype(jnp.bfloat16)
        got = jnp.dot(pick, tails[...], preferred_element_type=jnp.float32)
        extras[...] = got.reshape(REQUESTS, 16, WIDTH).astype(jnp.bfloat16)

    @pl.when(i >= 2)
    def _():
        for half in range(2):
            leave(i - 2, half).wait()

    row = lax.broadcasted_iota(jnp.int32, (KEYS, LANES), 0)
    positions = ((row & 7) << 6) + (row >> 3)
    for half, (keys, query) in enumerate(((keys0, query0), (keys1, query1))):
        request = staying_request(2 * i + half, me, index)
        extra = extras[request]
        visible = positions < lengths[me[0] * REQUESTS + request]
        scores = score(keys[0], visible, extra, joined(query))
        answer = answer_of(scores, keys[0, :, :KV_RANK], extra[:, :KV_RANK])
        answers[slot, half] = answer.reshape(STEPS, HEADS, KV_RANK)
    for half in range(2):
        leave(i, half).start()

    @pl.when(i == STAYING_STEPS - 1)
    def _():
        for step in range(STAYING_STEPS - 2, STAYING_STEPS):
            for half in range(2):
                leave(step, half).wait()


def staying(scalars, keys, queries, tails):
    def key_spec(half):
        return pl.BlockSpec(
            (1, KEYS, WIDTH),
            lambda i, me, lengths, index: (staying_request(2 * i + half, me, index), 0, 0),
        )

    def query_spec(half):
        return pl.BlockSpec(
            (STEPS, 1, WIDTH, HEADS),
            lambda i, me, lengths, index: (0, staying_request(2 * i + half, me, index), 0, 0),
        )

    return pl.pallas_call(
        staying_kernel,
        grid_spec=pltpu.PrefetchScalarGridSpec(
            num_scalar_prefetch=3,
            grid=(STAYING_STEPS,),
            in_specs=[
                key_spec(0),
                key_spec(1),
                query_spec(0),
                query_spec(1),
                pl.BlockSpec((STEPS * REQUESTS, WIDTH), lambda i, *_: (0, 0)),
            ],
            out_specs=pl.BlockSpec(memory_space=pl.ANY),
            scratch_shapes=[
                pltpu.VMEM((REQUESTS, 16, WIDTH), jnp.bfloat16),
                pltpu.VMEM((2, 2, STEPS, HEADS, KV_RANK), jnp.bfloat16),
                pltpu.SemaphoreType.DMA((2, 2)),
            ],
        ),
        out_shape=jax.ShapeDtypeStruct((STEPS, REQUESTS, HEADS, KV_RANK), jnp.bfloat16),
        compiler_params=pltpu.CompilerParams(vmem_limit_bytes=VMEM_BYTES),
        cost_estimate=pl.CostEstimate(
            flops=7_000_000_000, bytes_accessed=21_000_000, transcendentals=3_000_000
        ),
        name="staying",
    )(*scalars, keys, keys, queries, queries, tails)


def landing_kernel(me, index, shift, far, near, old, arrived, attended):
    del me, index, shift, old
    for k, got in enumerate((far, near)):

        @pl.when(pl.program_id(0) == k)
        def _(got=got):
            row = lax.broadcasted_iota(jnp.int32, (KEYS, KEYS), 0)
            column = lax.broadcasted_iota(jnp.int32, (KEYS, KEYS), 1)
            hit = column == ((row & 63) << 3) + (row >> 6)
            by_page = jnp.where(hit, 1.0, 0.0).astype(jnp.bfloat16)

            def turned(rows):
                block = jnp.dot(by_page, rows, preferred_element_type=jnp.float32)
                return block.astype(jnp.bfloat16).reshape(PAGES, TOKENS, rows.shape[1])

            arrived[:, :, :KV_RANK] = turned(
                jnp.concatenate(
                    [got[c * KEYS : (c + 1) * KEYS] for c in range(KV_RANK // LANES)], axis=1
                )
            )
            rope = got[4 * KEYS : PAGE_ROWS]
            arrived[:, :, KV_RANK:] = turned(
                jnp.concatenate([rope[:, :ROPE], rope[:, ROPE:]], axis=0)
            )
            for s in range(STEPS):
                for c in range(KV_RANK // LANES):
                    start = PAGE_ROWS + (s * 4 + c) * HEADS
                    attended[s, 0, :, c * LANES : (c + 1) * LANES] = got[start : start + HEADS]


def landing(scalars, far, near, attended):
    whole = pl.BlockSpec((PAYLOAD_ROWS, LANES), lambda i, *_: (0, 0))

    def mover(i, shift):
        last = near_mover(shift)
        return jnp.where(i == 1, last, 1 - last)

    return pl.pallas_call(
        landing_kernel,
        grid_spec=pltpu.PrefetchScalarGridSpec(
            num_scalar_prefetch=3,
            grid=(MOVERS,),
            in_specs=[whole] * 2 + [pl.BlockSpec(memory_space=pl.ANY)],
            out_specs=[
                pl.BlockSpec(
                    (PAGES, TOKENS, WIDTH), lambda i, me, index, shift: (mover(i, shift), 0, 0)
                ),
                pl.BlockSpec(
                    (STEPS, 1, HEADS, KV_RANK),
                    lambda i, me, index, shift: (
                        0,
                        index[me[0] * MOVERS + mover(i, shift)],
                        0,
                        0,
                    ),
                ),
            ],
        ),
        out_shape=[
            jax.ShapeDtypeStruct((MOVERS * PAGES, TOKENS, WIDTH), jnp.bfloat16),
            jax.ShapeDtypeStruct(attended.shape, attended.dtype),
        ],
        input_output_aliases={5: 1},
        compiler_params=pltpu.CompilerParams(vmem_limit_bytes=24 * 1024 * 1024),
        cost_estimate=pl.CostEstimate(flops=0, bytes_accessed=6_000_000, transcendentals=0),
        name="landing",
    )(*scalars, far, near, attended)


def choosing_kernel(shift, still, next_, last, far, near, sent):
    for k, out in enumerate((far, near)):
        rest = thirds(shift[slot_mover(k, shift)])[1]
        for value, source in ((0, still), (1, next_), (-1, last)):

            @pl.when(rest == value)
            def _(source=source, out=out, k=k):
                pltpu.make_async_copy(source.at[k], out, sent.at[k]).start()

    for k, out in enumerate((far, near)):
        pltpu.make_async_copy(still.at[k], out, sent.at[k]).wait()


def choosing(shift, still, next_, last):
    anywhere = pl.BlockSpec(memory_space=pl.ANY)
    payload = jax.ShapeDtypeStruct((PAYLOAD_ROWS, LANES), jnp.bfloat16)
    whole = pl.BlockSpec((PAYLOAD_ROWS, LANES), lambda i, *_: (0, 0))
    return pl.pallas_call(
        choosing_kernel,
        grid_spec=pltpu.PrefetchScalarGridSpec(
            num_scalar_prefetch=1,
            grid=(1,),
            in_specs=[anywhere] * 3,
            out_specs=[whole] * 2,
            scratch_shapes=[pltpu.SemaphoreType.DMA((MOVERS,))],
        ),
        out_shape=[payload, payload],
        cost_estimate=pl.CostEstimate(flops=0, bytes_accessed=4_000_000, transcendentals=0),
        name="choosing",
    )(shift, still, next_, last)


def in_hbm(array):
    return pltpu.with_memory_space_constraint(array, pltpu.HBM)


def moved(block, distance):
    count = lax.axis_size("dp")
    if distance % count == 0:
        return block
    return lax.ppermute(block, "dp", [(i, (i + distance) % count) for i in range(count)])


def moved_by(block, choice, distances):
    branches = [functools.partial(moved, distance=d) for d in distances]
    return lax.switch(choice, branches, block)


def shards(kv_pool, queries, new_kv, lengths, page_table, mover_index, mover_shift, mover_slots):
    me = lax.axis_index("dp").reshape(1)
    pool = in_hbm(jnp.transpose(kv_pool, (1, 2, 0)))
    turned = in_hbm(jnp.transpose(queries, (0, 1, 3, 2)))
    tails = in_hbm(new_kv.reshape(STEPS * REQUESTS, WIDTH))
    table = in_hbm(page_table.T)
    slots = in_hbm(mover_slots.T)
    lengths, mover_index, shift = map(in_hbm, (lengths, mover_index, mover_shift))
    keys, still, far_third, near_third = gathering(
        (me, lengths, table, mover_index, shift, slots), pool, table, turned, tails
    )
    next_ = moved(still, 1)
    last = moved(still, -1)
    attended = staying((me, lengths, mover_index), keys, turned, tails)
    next_, last, attended = lax.optimization_barrier((next_, last, attended))
    far, near = choosing(shift, still, next_, last)
    far = moved_by(
        far, far_third.reshape(()), [3 * c for c in range(-FAR_THIRDS, FAR_THIRDS + 1)]
    )

    def by_bits(near):
        del near
        rest = thirds(mover_shift[near_mover(mover_shift)])[1]
        near = moved_by(still[1], rest + 1, [-1, 0, 1])
        third = near_third.reshape(()) - FAR_THIRDS
        below = jnp.where(third < 0, 1, 0)
        near = moved_by(near, below, [0, -3 * FAR_THIRDS])
        third = third + FAR_THIRDS * below
        for bit in range(5):
            near = moved_by(near, (third >> bit) & 1, [0, 3 << bit])
        return near

    near = lax.cond(
        near_third.reshape(()) == FAR_THIRDS, lambda near: near, by_bits, near
    )
    arrived, attended = landing((me, mover_index, shift), far, near, attended)
    return attended, arrived


def solution(mesh):
    in_specs = (
        P("dp", None, None),
        P(None, "dp", None, None),
        P(None, "dp", None),
        P(),
        P("dp", None),
        P(),
        P(),
        P(),
    )
    out_specs = (P(None, "dp", None, None), P("dp", None, None))
    return jax.shard_map(shards, mesh=mesh, in_specs=in_specs, out_specs=out_specs, check_vma=False)
```

```python
import functools

import jax
import jax.numpy as jnp
from jax import lax
from jax.experimental import pallas as pl
from jax.experimental.pallas import tpu as pltpu
from jax.sharding import PartitionSpec as P

KV_RANK = 512
ROPE = 64
WIDTH = KV_RANK + ROPE
HEADS = 128
STEPS = 3
REQUESTS = 16
PAGES = 8
TOKENS = 64
KEYS = PAGES * TOKENS
MOVERS = 2
LANES = 128
GROUP = 16
GATHER_STEPS = TOKENS // GROUP
PAIR_ROWS = 2 * REQUESTS * PAGES
FAR_THIRDS = 21
PAGE_ROWS = KEYS * WIDTH // LANES
ANSWER_ROWS = STEPS * HEADS * KV_RANK // LANES
PAYLOAD_ROWS = PAGE_ROWS + ANSWER_ROWS
VMEM_BYTES = 56 * 1024 * 1024

LOG2_E = 1.4426950408889634

score_scale = 192.0 ** (-0.5)


def thirds(shift):
    back = jnp.where(shift > 64, 1, 0)
    third = lax.div(shift + 1 + back, 3) - 43 * back
    return third, shift - 128 * back - 3 * third


def near_mover(shift):
    ways = [jnp.abs(thirds(shift[i])[0]) for i in range(MOVERS)]
    return jnp.where(ways[0] < ways[1], 0, 1)


def slot_mover(slot, shift):
    near = near_mover(shift)
    return near if slot == 1 else 1 - near


def slot_request(slot, me, index, shift):
    return index[me[0] * MOVERS + slot_mover(slot, shift)]


def score(keys, visible, tail, query):
    scores = jnp.dot(keys, query, preferred_element_type=jnp.float32)
    scores = jnp.where(jnp.concatenate([visible] * STEPS, axis=1), scores, -jnp.inf)
    tail_scores = jnp.dot(tail, query, preferred_element_type=jnp.float32)
    tail_row = lax.broadcasted_iota(jnp.int32, tail_scores.shape, 0)
    step = lax.broadcasted_iota(jnp.int32, tail_scores.shape, 1) >> 7
    tail_scores = jnp.where(tail_row <= step, tail_scores, -jnp.inf)
    return jnp.concatenate([scores, tail_scores], axis=0)


def answer_of(scores, values, tail_values):
    largest = jnp.max(scores, axis=0, keepdims=True)
    weights = jnp.exp2((scores - largest) * (score_scale * LOG2_E))
    share = 1.0 / jnp.sum(weights, axis=0, keepdims=True)
    rounded = weights.astype(jnp.bfloat16)
    contract = (((0,), (0,)), ((), ()))
    summed = lax.dot_general(
        rounded[:KEYS], values, contract, preferred_element_type=jnp.float32
    ) + lax.dot_general(rounded[KEYS:], tail_values, contract, preferred_element_type=jnp.float32)
    columns = [
        jnp.transpose(jnp.broadcast_to(share[:, s * HEADS : (s + 1) * HEADS], (HEADS, HEADS)))[:, :1]
        for s in range(STEPS)
    ]
    return (summed * jnp.concatenate(columns, axis=0)).astype(jnp.bfloat16)


def tail_rows(tails, request):
    row = lax.broadcasted_iota(jnp.int32, (16, STEPS * REQUESTS), 0)
    column = lax.broadcasted_iota(jnp.int32, (16, STEPS * REQUESTS), 1)
    pick = jnp.where(column == row * REQUESTS + request, 1.0, 0.0).astype(jnp.bfloat16)
    return jnp.dot(pick, tails, preferred_element_type=jnp.float32).astype(jnp.bfloat16)


def joined(query_ref):
    return jnp.concatenate([query_ref[s, 0] for s in range(STEPS)], axis=1)


def gathering_kernel(
    me,
    lengths,
    table,
    index,
    shift,
    slots,
    pool,
    table_block,
    query0,
    query1,
    tails,
    keys,
    out,
    far_third,
    near_third,
    select,
    leaving,
    ready,
    sent,
):
    group = pl.program_id(0)
    movers = [slot_mover(k, shift) for k in range(MOVERS)]
    requests = [index[me[0] * MOVERS + m] for m in movers]
    spans = [lengths[me[0] * REQUESTS + r] for r in requests]
    places = [[slots[j, me[0] * MOVERS + m] for j in range(PAGES)] for m in movers]

    @pl.when(group == 0)
    def _():
        far_third[0] = thirds(shift[movers[0]])[0] + FAR_THIRDS
        near_third[0] = thirds(shift[movers[1]])[0] + FAR_THIRDS

        row = lax.broadcasted_iota(jnp.int32, (PAIR_ROWS, 1), 0) & ~PAGES
        owner = lax.broadcasted_iota(jnp.int32, (PAIR_ROWS, REQUESTS), 0) >> 4
        mine = owner == lax.broadcasted_iota(jnp.int32, (PAIR_ROWS, REQUESTS), 1)
        numbers = lax.dot_general(
            jnp.where(mine, 1.0, 0.0).astype(jnp.bfloat16),
            table_block[...].astype(jnp.float32).astype(jnp.bfloat16),
            (((1,), (1,)), ((), ())),
            preferred_element_type=jnp.float32,
        )
        place = lax.broadcasted_iota(jnp.int32, (PAIR_ROWS, PAGES), 0) & 7
        chosen = place == lax.broadcasted_iota(jnp.int32, (PAIR_ROWS, PAGES), 1)
        page = jnp.sum(jnp.where(chosen, numbers, 0.0), axis=1, keepdims=True).astype(jnp.int32)
        for k in range(MOVERS):
            for j in range(PAGES):
                number = jnp.where(j * TOKENS < spans[k], table[j, requests[k]], -1)
                here = row == requests[k] * (2 * PAGES) + places[k][j]
                page = jnp.where(here, number, page)
        column = lax.broadcasted_iota(jnp.int32, (PAIR_ROWS, 2 * LANES), 1)
        token = (lax.broadcasted_iota(jnp.int32, (PAIR_ROWS, 2 * LANES), 0) >> 3) & 1
        hit = ((column & 127) == page) & (token == column >> 7)
        select[...] = jnp.where(hit, 1.0, 0.0).astype(jnp.bfloat16)

    def leave(step):
        rows = pl.ds(pl.multiple_of(step * (GROUP * PAGES), GROUP * PAGES), GROUP * PAGES)
        return pltpu.make_async_copy(ready.at[step % 2], keys.at[:, rows], sent.at[step % 2])

    def pick(pages):
        return lax.dot_general(
            select[...], pages, (((1,), (1,)), ((), ())), preferred_element_type=jnp.float32
        )

    @pl.when((group >= 2) & (group < GATHER_STEPS))
    def _():
        leave(group - 2).wait()

    @pl.when(group < GATHER_STEPS)
    def _():
        slot = group % 2
        pairs = [
            jnp.concatenate([pool[2 * u], pool[2 * u + 1]], axis=1) for u in range(GROUP // 2)
        ]
        for first in range(0, GROUP // 2, 4):
            ropes = pick(
                jnp.concatenate([pairs[first + v][KV_RANK:] for v in range(4)], axis=0)
            ).astype(jnp.bfloat16)
            for v in range(4):
                rows = pl.ds((first + v) * 16, 16)
                latent = pick(pairs[first + v][:KV_RANK]).astype(jnp.bfloat16)
                ready[slot, :, rows, :KV_RANK] = latent.reshape(REQUESTS, 16, KV_RANK)
                rope = ropes[:, v * ROPE : (v + 1) * ROPE]
                ready[slot, :, rows, KV_RANK:] = rope.reshape(REQUESTS, 16, ROPE)
        start = pl.multiple_of(group * (GROUP * PAGES), GROUP * PAGES)
        for k in range(MOVERS):
            leaving[k, pl.ds(start, GROUP * PAGES), :] = ready[slot, requests[k]]
        leave(group).start()

    @pl.when(group == GATHER_STEPS)
    def _():
        row = lax.broadcasted_iota(jnp.int32, (KEYS, LANES), 0)
        scores, extra = [], []
        for k, query in enumerate((query0, query1)):
            spare = spans[k] - (row >> 3)
            first = jnp.zeros((PAGES, LANES), jnp.int32)
            page_row = lax.broadcasted_iota(jnp.int32, (PAGES, LANES), 0)
            for j in range(PAGES):
                first = jnp.where(page_row == places[k][j], j * TOKENS, first)
            visible = (jnp.broadcast_to(first, (TOKENS, PAGES, LANES)).reshape(KEYS, LANES)) < spare
            extra.append(tail_rows(tails[...], requests[k]))
            scores.append(score(leaving[k], visible, extra[k], joined(query)))
        for k in range(MOVERS):
            for c in range(KV_RANK // LANES):
                out[k, c * KEYS : (c + 1) * KEYS] = leaving[k, :, c * LANES : (c + 1) * LANES]
            rope = leaving[k, :, KV_RANK:]
            out[k, 4 * KEYS : PAGE_ROWS] = jnp.concatenate(
                [rope[: KEYS // 2], rope[KEYS // 2 :]], axis=1
            )
            answer = answer_of(scores[k], leaving[k, :, :KV_RANK], extra[k][:, :KV_RANK])
            for s in range(STEPS):
                for c in range(KV_RANK // LANES):
                    start = PAGE_ROWS + (s * 4 + c) * HEADS
                    out[k, start : start + HEADS] = answer[
                        s * HEADS : (s + 1) * HEADS, c * LANES : (c + 1) * LANES
                    ]
        leave(GATHER_STEPS - 2).wait()
        leave(GATHER_STEPS - 1).wait()


def gathering(scalars, pool, table, queries, tails):
    def query_spec(slot):
        return pl.BlockSpec(
            (STEPS, 1, WIDTH, HEADS),
            lambda i, me, lengths, table, index, shift, slots: (
                0,
                slot_request(slot, me, index, shift),
                0,
                0,
            ),
        )

    number = jax.ShapeDtypeStruct((1,), jnp.int32)
    return pl.pallas_call(
        gathering_kernel,
        grid_spec=pltpu.PrefetchScalarGridSpec(
            num_scalar_prefetch=6,
            grid=(GATHER_STEPS + 1,),
            in_specs=[
                pl.BlockSpec(
                    (GROUP, WIDTH, LANES), lambda i, *_: (jnp.minimum(i, GATHER_STEPS - 1), 0, 0)
                ),
                pl.BlockSpec((PAGES, REQUESTS), lambda i, *_: (0, 0)),
                query_spec(0),
                query_spec(1),
                pl.BlockSpec((STEPS * REQUESTS, WIDTH), lambda i, *_: (0, 0)),
            ],
            out_specs=[
                pl.BlockSpec(memory_space=pl.ANY),
                pl.BlockSpec(memory_space=pltpu.VMEM),
            ]
            + [pl.BlockSpec(memory_space=pltpu.SMEM)] * 2,
            scratch_shapes=[
                pltpu.VMEM((PAIR_ROWS, 2 * LANES), jnp.bfloat16),
                pltpu.VMEM((MOVERS, KEYS, WIDTH), jnp.bfloat16),
                pltpu.VMEM((2, REQUESTS, GROUP * PAGES, WIDTH), jnp.bfloat16),
                pltpu.SemaphoreType.DMA((2,)),
            ],
        ),
        out_shape=[
            jax.ShapeDtypeStruct((REQUESTS, KEYS, WIDTH), jnp.bfloat16),
            pltpu.VMEM((MOVERS, PAYLOAD_ROWS, LANES), jnp.bfloat16),
        ]
        + [number] * 2,
        compiler_params=pltpu.CompilerParams(vmem_limit_bytes=VMEM_BYTES),
        cost_estimate=pl.CostEstimate(
            flops=4_000_000_000, bytes_accessed=24_000_000, transcendentals=400_000
        ),
        name="gathering",
    )(*scalars, pool, table, queries, queries, tails)


STAYING = REQUESTS - MOVERS


STAYING_STEPS = STAYING // 2


def staying_request(i, me, index):
    first, second = index[me[0] * MOVERS], index[me[0] * MOVERS + 1]
    low, high = jnp.minimum(first, second), jnp.maximum(first, second)
    request = i + jnp.where(i >= low, 1, 0)
    return request + jnp.where(request >= high, 1, 0)


def staying_kernel(
    me, lengths, index, keys0, keys1, query0, query1, tails, out, extras, answers, sent
):
    i = pl.program_id(0)
    slot = i % 2

    def leave(step, half):
        return pltpu.make_async_copy(
            answers.at[step % 2, half],
            out.at[:, staying_request(2 * step + half, me, index)],
            sent.at[step % 2, half],
        )

    @pl.when(i == 0)
    def _():
        row = lax.broadcasted_iota(jnp.int32, (16 * REQUESTS, STEPS * REQUESTS), 0)
        column = lax.broadcasted_iota(jnp.int32, (16 * REQUESTS, STEPS * REQUESTS), 1)
        hit = column == ((row & 15) << 4) + (row >> 4)
        pick = jnp.where(hit, 1.0, 0.0).astype(jnp.bfloat16)
        got = jnp.dot(pick, tails[...], preferred_element_type=jnp.float32)
        extras[...] = got.reshape(REQUESTS, 16, WIDTH).astype(jnp.bfloat16)

    @pl.when(i >= 2)
    def _():
        for half in range(2):
            leave(i - 2, half).wait()

    row = lax.broadcasted_iota(jnp.int32, (KEYS, LANES), 0)
    positions = ((row & 7) << 6) + (row >> 3)
    for half, (keys, query) in enumerate(((keys0, query0), (keys1, query1))):
        request = staying_request(2 * i + half, me, index)
        extra = extras[request]
        visible = positions < lengths[me[0] * REQUESTS + request]
        scores = score(keys[0], visible, extra, joined(query))
        answer = answer_of(scores, keys[0, :, :KV_RANK], extra[:, :KV_RANK])
        answers[slot, half] = answer.reshape(STEPS, HEADS, KV_RANK)
    for half in range(2):
        leave(i, half).start()

    @pl.when(i == STAYING_STEPS - 1)
    def _():
        for step in range(STAYING_STEPS - 2, STAYING_STEPS):
            for half in range(2):
                leave(step, half).wait()


def staying(scalars, keys, queries, tails):
    def key_spec(half):
        return pl.BlockSpec(
            (1, KEYS, WIDTH),
            lambda i, me, lengths, index: (staying_request(2 * i + half, me, index), 0, 0),
        )

    def query_spec(half):
        return pl.BlockSpec(
            (STEPS, 1, WIDTH, HEADS),
            lambda i, me, lengths, index: (0, staying_request(2 * i + half, me, index), 0, 0),
        )

    return pl.pallas_call(
        staying_kernel,
        grid_spec=pltpu.PrefetchScalarGridSpec(
            num_scalar_prefetch=3,
            grid=(STAYING_STEPS,),
            in_specs=[
                key_spec(0),
                key_spec(1),
                query_spec(0),
                query_spec(1),
                pl.BlockSpec((STEPS * REQUESTS, WIDTH), lambda i, *_: (0, 0)),
            ],
            out_specs=pl.BlockSpec(memory_space=pl.ANY),
            scratch_shapes=[
                pltpu.VMEM((REQUESTS, 16, WIDTH), jnp.bfloat16),
                pltpu.VMEM((2, 2, STEPS, HEADS, KV_RANK), jnp.bfloat16),
                pltpu.SemaphoreType.DMA((2, 2)),
            ],
        ),
        out_shape=jax.ShapeDtypeStruct((STEPS, REQUESTS, HEADS, KV_RANK), jnp.bfloat16),
        compiler_params=pltpu.CompilerParams(vmem_limit_bytes=61 * 1024 * 1024),
        cost_estimate=pl.CostEstimate(
            flops=7_000_000_000, bytes_accessed=21_000_000, transcendentals=3_000_000
        ),
        name="staying",
    )(*scalars, keys, keys, queries, queries, tails)


def landing_kernel(me, index, shift, far, near, old, arrived, attended, by_page):
    del me, index, shift, old

    @pl.when(pl.program_id(0) == 0)
    def _():
        row = lax.broadcasted_iota(jnp.int32, (KEYS, KEYS), 0)
        column = lax.broadcasted_iota(jnp.int32, (KEYS, KEYS), 1)
        hit = column == ((row & 63) << 3) + (row >> 6)
        by_page[...] = jnp.where(hit, 1.0, 0.0).astype(jnp.bfloat16)

    for k, got in enumerate((far, near)):

        @pl.when(pl.program_id(0) == k)
        def _(got=got):
            def turned(rows):
                block = jnp.dot(by_page[...], rows, preferred_element_type=jnp.float32)
                return block.astype(jnp.bfloat16).reshape(PAGES, TOKENS, rows.shape[1])

            arrived[:, :, :KV_RANK] = turned(
                jnp.concatenate(
                    [got[c * KEYS : (c + 1) * KEYS] for c in range(KV_RANK // LANES)], axis=1
                )
            )
            rope = got[4 * KEYS : PAGE_ROWS]
            arrived[:, :, KV_RANK:] = turned(
                jnp.concatenate([rope[:, :ROPE], rope[:, ROPE:]], axis=0)
            )
            for s in range(STEPS):
                for c in range(KV_RANK // LANES):
                    start = PAGE_ROWS + (s * 4 + c) * HEADS
                    attended[s, 0, :, c * LANES : (c + 1) * LANES] = got[start : start + HEADS]


def landing(scalars, far, near, attended):
    whole = pl.BlockSpec((PAYLOAD_ROWS, LANES), lambda i, *_: (0, 0))

    def mover(i, shift):
        last = near_mover(shift)
        return jnp.where(i == 1, last, 1 - last)

    return pl.pallas_call(
        landing_kernel,
        grid_spec=pltpu.PrefetchScalarGridSpec(
            num_scalar_prefetch=3,
            grid=(MOVERS,),
            in_specs=[whole] * 2 + [pl.BlockSpec(memory_space=pl.ANY)],
            out_specs=[
                pl.BlockSpec(
                    (PAGES, TOKENS, WIDTH), lambda i, me, index, shift: (mover(i, shift), 0, 0)
                ),
                pl.BlockSpec(
                    (STEPS, 1, HEADS, KV_RANK),
                    lambda i, me, index, shift: (
                        0,
                        index[me[0] * MOVERS + mover(i, shift)],
                        0,
                        0,
                    ),
                ),
            ],
            scratch_shapes=[pltpu.VMEM((KEYS, KEYS), jnp.bfloat16)],
        ),
        out_shape=[
            jax.ShapeDtypeStruct((MOVERS * PAGES, TOKENS, WIDTH), jnp.bfloat16),
            jax.ShapeDtypeStruct(attended.shape, attended.dtype),
        ],
        input_output_aliases={5: 1},
        compiler_params=pltpu.CompilerParams(vmem_limit_bytes=24 * 1024 * 1024),
        cost_estimate=pl.CostEstimate(flops=0, bytes_accessed=6_000_000, transcendentals=0),
        name="landing",
    )(*scalars, far, near, attended)


def choosing_kernel(shift, still, next_, last, far, near, sent):
    for k, out in enumerate((far, near)):
        rest = thirds(shift[slot_mover(k, shift)])[1]
        for value, source in ((0, still), (1, next_), (-1, last)):

            @pl.when(rest == value)
            def _(source=source, out=out, k=k):
                pltpu.make_async_copy(source.at[k], out, sent.at[k]).start()

    for k, out in enumerate((far, near)):
        pltpu.make_async_copy(still.at[k], out, sent.at[k]).wait()


def choosing(shift, still, next_, last):
    anywhere = pl.BlockSpec(memory_space=pl.ANY)
    return pl.pallas_call(
        choosing_kernel,
        grid_spec=pltpu.PrefetchScalarGridSpec(
            num_scalar_prefetch=1,
            grid=(1,),
            in_specs=[anywhere] * 3,
            out_specs=[pl.BlockSpec(memory_space=pltpu.VMEM)] * 2,
            scratch_shapes=[pltpu.SemaphoreType.DMA((MOVERS,))],
        ),
        out_shape=[pltpu.VMEM((PAYLOAD_ROWS, LANES), jnp.bfloat16)] * 2,
        cost_estimate=pl.CostEstimate(flops=0, bytes_accessed=4_000_000, transcendentals=0),
        name="choosing",
    )(shift, still, next_, last)


def in_hbm(array):
    return pltpu.with_memory_space_constraint(array, pltpu.HBM)


def moved(block, distance):
    count = lax.axis_size("dp")
    if distance % count == 0:
        return block
    return lax.ppermute(block, "dp", [(i, (i + distance) % count) for i in range(count)])


def moved_by(block, choice, distances):
    branches = [functools.partial(moved, distance=d) for d in distances]
    return lax.switch(choice, branches, block)


def shards(kv_pool, queries, new_kv, lengths, page_table, mover_index, mover_shift, mover_slots):
    me = lax.axis_index("dp").reshape(1)
    pool = in_hbm(jnp.transpose(kv_pool, (1, 2, 0)))
    turned = in_hbm(jnp.transpose(queries, (0, 1, 3, 2)))
    tails = in_hbm(new_kv.reshape(STEPS * REQUESTS, WIDTH))
    table = in_hbm(page_table.T)
    slots = in_hbm(mover_slots.T)
    lengths, mover_index, shift = map(in_hbm, (lengths, mover_index, mover_shift))
    keys, still, far_third, near_third = gathering(
        (me, lengths, table, mover_index, shift, slots), pool, table, turned, tails
    )
    next_ = moved(still, 1)
    last = moved(still, -1)
    attended = staying((me, lengths, mover_index), keys, turned, tails)
    next_, last, attended = lax.optimization_barrier((next_, last, attended))
    far, near = choosing(shift, still, next_, last)
    far = moved_by(
        far, far_third.reshape(()), [3 * c for c in range(-FAR_THIRDS, FAR_THIRDS + 1)]
    )

    def by_bits(near):
        del near
        rest = thirds(mover_shift[near_mover(mover_shift)])[1]
        near = moved_by(still[1], rest + 1, [-1, 0, 1])
        third = near_third.reshape(()) - FAR_THIRDS
        below = jnp.where(third < 0, 1, 0)
        near = moved_by(near, below, [0, -3 * FAR_THIRDS])
        third = third + FAR_THIRDS * below
        for bit in range(5):
            near = moved_by(near, (third >> bit) & 1, [0, 3 << bit])
        return near

    near = lax.cond(
        near_third.reshape(()) == FAR_THIRDS, lambda near: near, by_bits, near
    )
    arrived, attended = landing((me, mover_index, shift), far, near, attended)
    return attended, arrived


def solution(mesh):
    in_specs = (
        P("dp", None, None),
        P(None, "dp", None, None),
        P(None, "dp", None),
        P(),
        P("dp", None),
        P(),
        P(),
        P(),
    )
    out_specs = (P(None, "dp", None, None), P("dp", None, None))
    return jax.shard_map(shards, mesh=mesh, in_specs=in_specs, out_specs=out_specs, check_vma=False)
```

```python
import functools

import jax
import jax.numpy as jnp
from jax import lax
from jax.experimental import pallas as pl
from jax.experimental.pallas import tpu as pltpu
from jax.sharding import PartitionSpec as P

KV_RANK = 512
ROPE = 64
WIDTH = KV_RANK + ROPE
HEADS = 128
STEPS = 3
REQUESTS = 16
PAGES = 8
TOKENS = 64
KEYS = PAGES * TOKENS
MOVERS = 2
LANES = 128
GROUP = 16
GATHER_STEPS = TOKENS // GROUP
PAIR_ROWS = 2 * REQUESTS * PAGES
FAR_THIRDS = 21
NEAR, RESTS, LEAVING, LENGTHS, FACTS = 0, 1, 3, 8, 32
PAGE_ROWS = KEYS * WIDTH // LANES
ANSWER_ROWS = STEPS * HEADS * KV_RANK // LANES
PAYLOAD_ROWS = PAGE_ROWS + ANSWER_ROWS
VMEM_BYTES = 56 * 1024 * 1024

LOG2_E = 1.4426950408889634

score_scale = 192.0 ** (-0.5)


def thirds(shift):
    back = jnp.where(shift > 64, 1, 0)
    third = lax.div(shift + 1 + back, 3) - 43 * back
    return third, shift - 128 * back - 3 * third


def near_mover(shift):
    ways = [jnp.abs(thirds(shift[i])[0]) for i in range(MOVERS)]
    return jnp.where(ways[0] < ways[1], 0, 1)


def slot_mover(slot, shift):
    near = near_mover(shift)
    return near if slot == 1 else 1 - near


def slot_request(slot, me, index, shift):
    return index[me[0] * MOVERS + slot_mover(slot, shift)]


def score(keys, visible, tail, query):
    scores = jnp.dot(keys, query, preferred_element_type=jnp.float32)
    scores = jnp.where(jnp.concatenate([visible] * STEPS, axis=1), scores, -jnp.inf)
    tail_scores = jnp.dot(tail, query, preferred_element_type=jnp.float32)
    tail_row = lax.broadcasted_iota(jnp.int32, tail_scores.shape, 0)
    step = lax.broadcasted_iota(jnp.int32, tail_scores.shape, 1) >> 7
    tail_scores = jnp.where(tail_row <= step, tail_scores, -jnp.inf)
    return jnp.concatenate([scores, tail_scores], axis=0)


def answer_of(scores, values, tail_values):
    largest = jnp.max(scores, axis=0, keepdims=True)
    weights = jnp.exp2((scores - largest) * (score_scale * LOG2_E))
    share = 1.0 / jnp.sum(weights, axis=0, keepdims=True)
    rounded = weights.astype(jnp.bfloat16)
    contract = (((0,), (0,)), ((), ()))
    summed = lax.dot_general(
        rounded[:KEYS], values, contract, preferred_element_type=jnp.float32
    ) + lax.dot_general(rounded[KEYS:], tail_values, contract, preferred_element_type=jnp.float32)
    columns = [
        jnp.transpose(jnp.broadcast_to(share[:, s * HEADS : (s + 1) * HEADS], (HEADS, HEADS)))[:, :1]
        for s in range(STEPS)
    ]
    return (summed * jnp.concatenate(columns, axis=0)).astype(jnp.bfloat16)


def tail_rows(tails, request):
    row = lax.broadcasted_iota(jnp.int32, (16, STEPS * REQUESTS), 0)
    column = lax.broadcasted_iota(jnp.int32, (16, STEPS * REQUESTS), 1)
    pick = jnp.where(column == row * REQUESTS + request, 1.0, 0.0).astype(jnp.bfloat16)
    return jnp.dot(pick, tails, preferred_element_type=jnp.float32).astype(jnp.bfloat16)


def joined(query_ref):
    return jnp.concatenate([query_ref[s, 0] for s in range(STEPS)], axis=1)


def gathering_kernel(
    me,
    lengths,
    table,
    index,
    shift,
    slots,
    pool,
    table_block,
    query0,
    query1,
    tails,
    keys,
    out,
    far_third,
    near_third,
    facts,
    select,
    leaving,
    ready,
    sent,
):
    group = pl.program_id(0)
    movers = [slot_mover(k, shift) for k in range(MOVERS)]
    requests = [index[me[0] * MOVERS + m] for m in movers]
    spans = [lengths[me[0] * REQUESTS + r] for r in requests]
    places = [[slots[j, me[0] * MOVERS + m] for j in range(PAGES)] for m in movers]

    @pl.when(group == 0)
    def _():
        far_third[0] = thirds(shift[movers[0]])[0] + FAR_THIRDS
        near_third[0] = thirds(shift[movers[1]])[0] + FAR_THIRDS
        facts[NEAR] = movers[1]
        for k in range(MOVERS):
            facts[RESTS + k] = thirds(shift[movers[k]])[1]
            facts[LEAVING + k] = index[me[0] * MOVERS + k]
        for r in range(REQUESTS):
            facts[LENGTHS + r] = lengths[me[0] * REQUESTS + r]

        row = lax.broadcasted_iota(jnp.int32, (PAIR_ROWS, 1), 0) & ~PAGES
        owner = lax.broadcasted_iota(jnp.int32, (PAIR_ROWS, REQUESTS), 0) >> 4
        mine = owner == lax.broadcasted_iota(jnp.int32, (PAIR_ROWS, REQUESTS), 1)
        numbers = lax.dot_general(
            jnp.where(mine, 1.0, 0.0).astype(jnp.bfloat16),
            table_block[...].astype(jnp.float32).astype(jnp.bfloat16),
            (((1,), (1,)), ((), ())),
            preferred_element_type=jnp.float32,
        )
        place = lax.broadcasted_iota(jnp.int32, (PAIR_ROWS, PAGES), 0) & 7
        chosen = place == lax.broadcasted_iota(jnp.int32, (PAIR_ROWS, PAGES), 1)
        page = jnp.sum(jnp.where(chosen, numbers, 0.0), axis=1, keepdims=True).astype(jnp.int32)
        for k in range(MOVERS):
            for j in range(PAGES):
                number = jnp.where(j * TOKENS < spans[k], table[j, requests[k]], -1)
                here = row == requests[k] * (2 * PAGES) + places[k][j]
                page = jnp.where(here, number, page)
        column = lax.broadcasted_iota(jnp.int32, (PAIR_ROWS, 2 * LANES), 1)
        token = (lax.broadcasted_iota(jnp.int32, (PAIR_ROWS, 2 * LANES), 0) >> 3) & 1
        hit = ((column & 127) == page) & (token == column >> 7)
        select[...] = jnp.where(hit, 1.0, 0.0).astype(jnp.bfloat16)

    def leave(step):
        rows = pl.ds(pl.multiple_of(step * (GROUP * PAGES), GROUP * PAGES), GROUP * PAGES)
        return pltpu.make_async_copy(ready.at[step % 2], keys.at[:, rows], sent.at[step % 2])

    def pick(pages):
        return lax.dot_general(
            select[...], pages, (((1,), (1,)), ((), ())), preferred_element_type=jnp.float32
        )

    @pl.when((group >= 2) & (group < GATHER_STEPS))
    def _():
        leave(group - 2).wait()

    @pl.when(group < GATHER_STEPS)
    def _():
        slot = group % 2
        pairs = [
            jnp.concatenate([pool[2 * u], pool[2 * u + 1]], axis=1) for u in range(GROUP // 2)
        ]
        for first in range(0, GROUP // 2, 4):
            ropes = pick(
                jnp.concatenate([pairs[first + v][KV_RANK:] for v in range(4)], axis=0)
            ).astype(jnp.bfloat16)
            for v in range(4):
                rows = pl.ds((first + v) * 16, 16)
                latent = pick(pairs[first + v][:KV_RANK]).astype(jnp.bfloat16)
                ready[slot, :, rows, :KV_RANK] = latent.reshape(REQUESTS, 16, KV_RANK)
                rope = ropes[:, v * ROPE : (v + 1) * ROPE]
                ready[slot, :, rows, KV_RANK:] = rope.reshape(REQUESTS, 16, ROPE)
        start = pl.multiple_of(group * (GROUP * PAGES), GROUP * PAGES)
        for k in range(MOVERS):
            leaving[k, pl.ds(start, GROUP * PAGES), :] = ready[slot, requests[k]]
        leave(group).start()

    @pl.when(group == GATHER_STEPS)
    def _():
        row = lax.broadcasted_iota(jnp.int32, (KEYS, LANES), 0)
        scores, extra = [], []
        for k, query in enumerate((query0, query1)):
            spare = spans[k] - (row >> 3)
            first = jnp.zeros((PAGES, LANES), jnp.int32)
            page_row = lax.broadcasted_iota(jnp.int32, (PAGES, LANES), 0)
            for j in range(PAGES):
                first = jnp.where(page_row == places[k][j], j * TOKENS, first)
            visible = (jnp.broadcast_to(first, (TOKENS, PAGES, LANES)).reshape(KEYS, LANES)) < spare
            extra.append(tail_rows(tails[...], requests[k]))
            scores.append(score(leaving[k], visible, extra[k], joined(query)))
        for k in range(MOVERS):
            for c in range(KV_RANK // LANES):
                out[k, c * KEYS : (c + 1) * KEYS] = leaving[k, :, c * LANES : (c + 1) * LANES]
            rope = leaving[k, :, KV_RANK:]
            out[k, 4 * KEYS : PAGE_ROWS] = jnp.concatenate(
                [rope[: KEYS // 2], rope[KEYS // 2 :]], axis=1
            )
            answer = answer_of(scores[k], leaving[k, :, :KV_RANK], extra[k][:, :KV_RANK])
            for s in range(STEPS):
                for c in range(KV_RANK // LANES):
                    start = PAGE_ROWS + (s * 4 + c) * HEADS
                    out[k, start : start + HEADS] = answer[
                        s * HEADS : (s + 1) * HEADS, c * LANES : (c + 1) * LANES
                    ]
        leave(GATHER_STEPS - 2).wait()
        leave(GATHER_STEPS - 1).wait()


def gathering(scalars, pool, table, queries, tails):
    def query_spec(slot):
        return pl.BlockSpec(
            (STEPS, 1, WIDTH, HEADS),
            lambda i, me, lengths, table, index, shift, slots: (
                0,
                slot_request(slot, me, index, shift),
                0,
                0,
            ),
        )

    number = jax.ShapeDtypeStruct((1,), jnp.int32)
    return pl.pallas_call(
        gathering_kernel,
        grid_spec=pltpu.PrefetchScalarGridSpec(
            num_scalar_prefetch=6,
            grid=(GATHER_STEPS + 1,),
            in_specs=[
                pl.BlockSpec(
                    (GROUP, WIDTH, LANES), lambda i, *_: (jnp.minimum(i, GATHER_STEPS - 1), 0, 0)
                ),
                pl.BlockSpec((PAGES, REQUESTS), lambda i, *_: (0, 0)),
                query_spec(0),
                query_spec(1),
                pl.BlockSpec((STEPS * REQUESTS, WIDTH), lambda i, *_: (0, 0)),
            ],
            out_specs=[
                pl.BlockSpec(memory_space=pl.ANY),
                pl.BlockSpec(memory_space=pltpu.VMEM),
            ]
            + [pl.BlockSpec(memory_space=pltpu.SMEM)] * 3,
            scratch_shapes=[
                pltpu.VMEM((PAIR_ROWS, 2 * LANES), jnp.bfloat16),
                pltpu.VMEM((MOVERS, KEYS, WIDTH), jnp.bfloat16),
                pltpu.VMEM((2, REQUESTS, GROUP * PAGES, WIDTH), jnp.bfloat16),
                pltpu.SemaphoreType.DMA((2,)),
            ],
        ),
        out_shape=[
            jax.ShapeDtypeStruct((REQUESTS, KEYS, WIDTH), jnp.bfloat16),
            pltpu.VMEM((MOVERS, PAYLOAD_ROWS, LANES), jnp.bfloat16),
        ]
        + [number] * 2
        + [jax.ShapeDtypeStruct((FACTS,), jnp.int32)],
        compiler_params=pltpu.CompilerParams(vmem_limit_bytes=VMEM_BYTES),
        cost_estimate=pl.CostEstimate(
            flops=4_000_000_000, bytes_accessed=24_000_000, transcendentals=400_000
        ),
        name="gathering",
    )(*scalars, pool, table, queries, queries, tails)


STAYING = REQUESTS - MOVERS


STAYING_STEPS = STAYING // 2


def staying_request(i, facts):
    first, second = facts[LEAVING], facts[LEAVING + 1]
    low, high = jnp.minimum(first, second), jnp.maximum(first, second)
    request = i + jnp.where(i >= low, 1, 0)
    return request + jnp.where(request >= high, 1, 0)


def staying_kernel(
    facts, keys0, keys1, query0, query1, tails, out, extras, answers, sent
):
    i = pl.program_id(0)
    slot = i % 2

    def leave(step, half):
        return pltpu.make_async_copy(
            answers.at[step % 2, half],
            out.at[:, staying_request(2 * step + half, facts)],
            sent.at[step % 2, half],
        )

    @pl.when(i == 0)
    def _():
        row = lax.broadcasted_iota(jnp.int32, (16 * REQUESTS, STEPS * REQUESTS), 0)
        column = lax.broadcasted_iota(jnp.int32, (16 * REQUESTS, STEPS * REQUESTS), 1)
        hit = column == ((row & 15) << 4) + (row >> 4)
        pick = jnp.where(hit, 1.0, 0.0).astype(jnp.bfloat16)
        got = jnp.dot(pick, tails[...], preferred_element_type=jnp.float32)
        extras[...] = got.reshape(REQUESTS, 16, WIDTH).astype(jnp.bfloat16)

    @pl.when(i >= 2)
    def _():
        for half in range(2):
            leave(i - 2, half).wait()

    row = lax.broadcasted_iota(jnp.int32, (KEYS, LANES), 0)
    positions = ((row & 7) << 6) + (row >> 3)
    for half, (keys, query) in enumerate(((keys0, query0), (keys1, query1))):
        request = staying_request(2 * i + half, facts)
        extra = extras[request]
        visible = positions < facts[LENGTHS + request]
        scores = score(keys[0], visible, extra, joined(query))
        answer = answer_of(scores, keys[0, :, :KV_RANK], extra[:, :KV_RANK])
        answers[slot, half] = answer.reshape(STEPS, HEADS, KV_RANK)
    for half in range(2):
        leave(i, half).start()

    @pl.when(i == STAYING_STEPS - 1)
    def _():
        for step in range(STAYING_STEPS - 2, STAYING_STEPS):
            for half in range(2):
                leave(step, half).wait()


def staying(facts, keys, queries, tails):
    def key_spec(half):
        return pl.BlockSpec(
            (1, KEYS, WIDTH),
            lambda i, facts: (staying_request(2 * i + half, facts), 0, 0),
        )

    def query_spec(half):
        return pl.BlockSpec(
            (STEPS, 1, WIDTH, HEADS),
            lambda i, facts: (0, staying_request(2 * i + half, facts), 0, 0),
        )

    return pl.pallas_call(
        staying_kernel,
        grid_spec=pltpu.PrefetchScalarGridSpec(
            num_scalar_prefetch=1,
            grid=(STAYING_STEPS,),
            in_specs=[
                key_spec(0),
                key_spec(1),
                query_spec(0),
                query_spec(1),
                pl.BlockSpec((STEPS * REQUESTS, WIDTH), lambda i, *_: (0, 0)),
            ],
            out_specs=pl.BlockSpec(memory_space=pl.ANY),
            scratch_shapes=[
                pltpu.VMEM((REQUESTS, 16, WIDTH), jnp.bfloat16),
                pltpu.VMEM((2, 2, STEPS, HEADS, KV_RANK), jnp.bfloat16),
                pltpu.SemaphoreType.DMA((2, 2)),
            ],
        ),
        out_shape=jax.ShapeDtypeStruct((STEPS, REQUESTS, HEADS, KV_RANK), jnp.bfloat16),
        compiler_params=pltpu.CompilerParams(vmem_limit_bytes=61 * 1024 * 1024),
        cost_estimate=pl.CostEstimate(
            flops=7_000_000_000, bytes_accessed=21_000_000, transcendentals=3_000_000
        ),
        name="staying",
    )(facts, keys, keys, queries, queries, tails)


def landing_kernel(facts, far, near, old, arrived, attended, by_page):
    del facts, old

    @pl.when(pl.program_id(0) == 0)
    def _():
        row = lax.broadcasted_iota(jnp.int32, (KEYS, KEYS), 0)
        column = lax.broadcasted_iota(jnp.int32, (KEYS, KEYS), 1)
        hit = column == ((row & 63) << 3) + (row >> 6)
        by_page[...] = jnp.where(hit, 1.0, 0.0).astype(jnp.bfloat16)

    for k, got in enumerate((far, near)):

        @pl.when(pl.program_id(0) == k)
        def _(got=got):
            def turned(rows):
                block = jnp.dot(by_page[...], rows, preferred_element_type=jnp.float32)
                return block.astype(jnp.bfloat16).reshape(PAGES, TOKENS, rows.shape[1])

            arrived[:, :, :KV_RANK] = turned(
                jnp.concatenate(
                    [got[c * KEYS : (c + 1) * KEYS] for c in range(KV_RANK // LANES)], axis=1
                )
            )
            rope = got[4 * KEYS : PAGE_ROWS]
            arrived[:, :, KV_RANK:] = turned(
                jnp.concatenate([rope[:, :ROPE], rope[:, ROPE:]], axis=0)
            )
            for s in range(STEPS):
                for c in range(KV_RANK // LANES):
                    start = PAGE_ROWS + (s * 4 + c) * HEADS
                    attended[s, 0, :, c * LANES : (c + 1) * LANES] = got[start : start + HEADS]


def landing(facts, far, near, attended):
    whole = pl.BlockSpec((PAYLOAD_ROWS, LANES), lambda i, *_: (0, 0))

    def mover(i, facts):
        return jnp.where(i == 1, facts[NEAR], 1 - facts[NEAR])

    return pl.pallas_call(
        landing_kernel,
        grid_spec=pltpu.PrefetchScalarGridSpec(
            num_scalar_prefetch=1,
            grid=(MOVERS,),
            in_specs=[whole] * 2 + [pl.BlockSpec(memory_space=pl.ANY)],
            out_specs=[
                pl.BlockSpec(
                    (PAGES, TOKENS, WIDTH), lambda i, facts: (mover(i, facts), 0, 0)
                ),
                pl.BlockSpec(
                    (STEPS, 1, HEADS, KV_RANK),
                    lambda i, facts: (0, facts[LEAVING + mover(i, facts)], 0, 0),
                ),
            ],
            scratch_shapes=[pltpu.VMEM((KEYS, KEYS), jnp.bfloat16)],
        ),
        out_shape=[
            jax.ShapeDtypeStruct((MOVERS * PAGES, TOKENS, WIDTH), jnp.bfloat16),
            jax.ShapeDtypeStruct(attended.shape, attended.dtype),
        ],
        input_output_aliases={3: 1},
        compiler_params=pltpu.CompilerParams(vmem_limit_bytes=24 * 1024 * 1024),
        cost_estimate=pl.CostEstimate(flops=0, bytes_accessed=6_000_000, transcendentals=0),
        name="landing",
    )(facts, far, near, attended)


def choosing_kernel(facts, still, next_, last, far, near, sent):
    for k, out in enumerate((far, near)):
        rest = facts[RESTS + k]
        for value, source in ((0, still), (1, next_), (-1, last)):

            @pl.when(rest == value)
            def _(source=source, out=out, k=k):
                pltpu.make_async_copy(source.at[k], out, sent.at[k]).start()

    for k, out in enumerate((far, near)):
        pltpu.make_async_copy(still.at[k], out, sent.at[k]).wait()


def choosing(facts, still, next_, last):
    anywhere = pl.BlockSpec(memory_space=pl.ANY)
    return pl.pallas_call(
        choosing_kernel,
        grid_spec=pltpu.PrefetchScalarGridSpec(
            num_scalar_prefetch=1,
            grid=(1,),
            in_specs=[anywhere] * 3,
            out_specs=[pl.BlockSpec(memory_space=pltpu.VMEM)] * 2,
            scratch_shapes=[pltpu.SemaphoreType.DMA((MOVERS,))],
        ),
        out_shape=[pltpu.VMEM((PAYLOAD_ROWS, LANES), jnp.bfloat16)] * 2,
        cost_estimate=pl.CostEstimate(flops=0, bytes_accessed=4_000_000, transcendentals=0),
        name="choosing",
    )(facts, still, next_, last)


def in_hbm(array):
    return pltpu.with_memory_space_constraint(array, pltpu.HBM)


def moved(block, distance):
    count = lax.axis_size("dp")
    if distance % count == 0:
        return block
    return lax.ppermute(block, "dp", [(i, (i + distance) % count) for i in range(count)])


def moved_by(block, choice, distances):
    branches = [functools.partial(moved, distance=d) for d in distances]
    return lax.switch(choice, branches, block)


def shards(kv_pool, queries, new_kv, lengths, page_table, mover_index, mover_shift, mover_slots):
    me = lax.axis_index("dp").reshape(1)
    pool = in_hbm(jnp.transpose(kv_pool, (1, 2, 0)))
    turned = in_hbm(jnp.transpose(queries, (0, 1, 3, 2)))
    tails = in_hbm(new_kv.reshape(STEPS * REQUESTS, WIDTH))
    table = in_hbm(page_table.T)
    slots = in_hbm(mover_slots.T)
    lengths, mover_index, shift = map(in_hbm, (lengths, mover_index, mover_shift))
    keys, still, far_third, near_third, facts = gathering(
        (me, lengths, table, mover_index, shift, slots), pool, table, turned, tails
    )
    last = moved(still, -1)
    next_ = moved(still, 1)
    facts = in_hbm(facts)
    attended = staying(facts, keys, turned, tails)
    last, next_, attended = lax.optimization_barrier((last, next_, attended))
    far, near = choosing(facts, still, next_, last)
    far = moved_by(
        far, far_third.reshape(()), [3 * c for c in range(-FAR_THIRDS, FAR_THIRDS + 1)]
    )

    def by_bits(near):
        del near
        rest = thirds(mover_shift[near_mover(mover_shift)])[1]
        near = moved_by(still[1], rest + 1, [-1, 0, 1])
        third = near_third.reshape(()) - FAR_THIRDS
        below = jnp.where(third < 0, 1, 0)
        near = moved_by(near, below, [0, -3 * FAR_THIRDS])
        third = third + FAR_THIRDS * below
        for bit in range(5):
            near = moved_by(near, (third >> bit) & 1, [0, 3 << bit])
        return near

    arrived, attended = lax.cond(
        near_third.reshape(()) == FAR_THIRDS,
        lambda far, near, attended: landing(facts, far, near, attended),
        lambda far, near, attended: landing(facts, far, by_bits(near), attended),
        far,
        near,
        attended,
    )
    return attended, arrived


def solution(mesh):
    in_specs = (
        P("dp", None, None),
        P(None, "dp", None, None),
        P(None, "dp", None),
        P(),
        P("dp", None),
        P(),
        P(),
        P(),
    )
    out_specs = (P(None, "dp", None, None), P("dp", None, None))
    return jax.shard_map(shards, mesh=mesh, in_specs=in_specs, out_specs=out_specs, check_vma=False)
```
